32 devices in a mesh: dp: 16 (over z, y, x), tensor: 2 (over core).
Axes of the slice: x: 2, y: 2, z: 4, core: 2. Of those that a mesh axis runs over, the one named last changes fastest.
Arguments:
- inputs: bfloat16 [16384, 1152], P(('dp', 'tensor')), may hold values from -6 to 6
- segments: int32 [16, 1024], P('dp'), may hold values from 0 to 2, as said below
- positions: int32 [16, 1024], P('dp'), may hold values from 0 to 5119, as said below
- query_weight: bfloat16 [1152, 1024], P('dp', 'tensor'), may hold values from -0.1875 to 0.1875
- key_weight: bfloat16 [1152, 256], P('dp'), may hold values from -0.1875 to 0.1875
- value_weight: bfloat16 [1152, 256], P('dp'), may hold values from -0.1875 to 0.1875
- output_weight: bfloat16 [1152, 1024], P('dp', 'tensor'), may hold values from -0.1875 to 0.1875
- gain_attn_in: bfloat16 [1152], P('dp'), may hold values from 0.099609375 to 1.8984375
- gain_attn_out: bfloat16 [1152], P('dp'), may hold values from 0.099609375 to 1.8984375
- gain_query: bfloat16 [256], P('dp'), may hold values from 0.099609375 to 1.8984375
- gain_key: bfloat16 [256], P('dp'), may hold values from 0.099609375 to 1.8984375
- gate_weight: bfloat16 [1152, 6912], P('dp', 'tensor'), may hold values from -0.1875 to 0.1875
- up_weight: bfloat16 [1152, 6912], P('dp', 'tensor'), may hold values from -0.1875 to 0.1875
- down_weight: bfloat16 [1152, 6912], P('dp', 'tensor'), may hold values from -0.078125 to 0.078125
- gain_ffn_in: bfloat16 [1152], P('dp'), may hold values from 0.099609375 to 1.8984375
- gain_ffn_out: bfloat16 [1152], P('dp'), may hold values from 0.099609375 to 1.8984375
- cotangent: bfloat16 [16384, 1152], P(('dp', 'tensor')), may hold values from -6 to 6
Outputs:
- layer_out: bfloat16 [16384, 1152], P(('dp', 'tensor'))
- input_grad: float32 [16384, 1152], P(('dp', 'tensor'))
- query_weight_grad: float32 [1152, 1024], P('dp', 'tensor')
- key_weight_grad: float32 [1152, 256], P(('dp', 'tensor'))
- value_weight_grad: float32 [1152, 256], P(('dp', 'tensor'))
- output_weight_grad: float32 [1152, 1024], P('dp', 'tensor')
- gain_attn_in_grad: float32 [1152], P(('dp', 'tensor'))
- gain_attn_out_grad: float32 [1152], P(('dp', 'tensor'))
- gain_query_grad: float32 [256], P(('dp', 'tensor'))
- gain_key_grad: float32 [256], P(('dp', 'tensor'))
- gate_weight_grad: float32 [1152, 6912], P('dp', 'tensor')
- up_weight_grad: float32 [1152, 6912], P('dp', 'tensor')
- down_weight_grad: float32 [1152, 6912], P('dp', 'tensor')
- gain_ffn_in_grad: float32 [1152], P(('dp', 'tensor'))
- gain_ffn_out_grad: float32 [1152], P(('dp', 'tensor'))
The draws below stay inside these ranges and needn't reach their ends.
Inputs may be any that keep to these rules, and one draw needn't show every extreme that they name: `segments`: document numbers never fall along a sequence; each sequence holds documents 0, 1 and 2. Within a document positions rise by one from token to token; document 0 starts at 0; the last token of every sequence has position 5119.
All inputs are finite; a program needn't handle non-finite values.
Results may differ from the reference program's by a relative error of at most 0.02.
Values may be sent and summed in bfloat16 or wider, within the bound.
A program may use at most 256 MiB of HBM per device.

```python
import math
import jax
import jax.numpy as jnp
from jax import lax

D = 1152
HEADS = 4
HD = 256
FF = 6912
WINDOW = 512
SEQ = 1024
GROUPS = 16
TOKENS = 16384


def doc_cuts(key):
    first_key, second_key = jax.random.split(key)
    first_cut = jax.random.randint(first_key, (GROUPS, 1), 1, SEQ // 4)
    second_cut = jax.random.randint(second_key, (GROUPS, 1), 3 * SEQ // 4, SEQ)
    return (first_cut, second_cut)


def draw_segments(key, part):
    first_cut, second_cut = doc_cuts(key)
    token_index = jnp.arange(SEQ, dtype=jnp.int32)[None, :]
    return (token_index >= first_cut).astype(jnp.int32) + (token_index >= second_cut).astype(jnp.int32)


def draw_positions(key, part):
    first_cut, second_cut = doc_cuts(key)
    key = jax.random.fold_in(key, 23)
    middle_offset = jax.random.randint(key, (GROUPS, 1), 0, 4096)
    token_index = jnp.arange(SEQ, dtype=jnp.int32)[None, :]
    in_second = token_index >= first_cut
    in_third = token_index >= second_cut
    first_doc = token_index
    second_doc = token_index - first_cut + middle_offset
    third_doc = token_index + 4096
    return jnp.where(in_third, third_doc, jnp.where(in_second, second_doc, first_doc)).astype(jnp.int32)


def level_of(stream_key, shape, cuts, smallest, high):
    gain = 1.0
    for dim, blocks in cuts:
        steps = jax.random.uniform(jax.random.fold_in(jax.random.fold_in(stream_key, 6), dim), (blocks,), jnp.float32, smallest / len(cuts), high / len(cuts))
        gain = gain * jnp.repeat(jnp.exp(steps), shape[dim] // blocks).reshape((-1,) + (1,) * (len(shape) - 1 - dim))
    return gain


def bell_draw(key, dims, scale, most, cuts=(), kind=jnp.bfloat16):
    values = jax.random.normal(key, dims, jnp.float32) * scale
    if len(cuts) > 0:
        values = level_of(key, dims, cuts, -0.22, 0.18) * values
    return jnp.clip(values, min=-most, max=most).astype(kind)


def setup_inputs(seed: int = 0) -> dict:
    splits = jax.random.split(jax.random.key(seed), 18)
    return {
        "inputs": bell_draw(splits[0], (TOKENS, D), 1.0, 6.0, ((0, 32),)),
        "segments": draw_segments(jax.random.fold_in(splits[17], 71), 0),
        "positions": draw_positions(jax.random.fold_in(splits[17], 71), 0),
        "query_weight": bell_draw(splits[3], (D, HEADS * HD), D ** -0.5, 0.1875, ((0, 16), (1, 2))),
        "key_weight": bell_draw(splits[4], (D, HD), D ** -0.5, 0.1875, ((0, 16),)),
        "value_weight": bell_draw(splits[5], (D, HD), D ** -0.5, 0.1875, ((0, 16),)),
        "output_weight": bell_draw(splits[6], (D, HEADS * HD), (HEADS * HD) ** -0.5, 0.1875, ((0, 16), (1, 2))),
        "gain_attn_in": jnp.clip(1.0 + 0.18 * jax.random.normal(splits[7], (D,), jnp.float32), 0.099609375, 1.8984375).astype(jnp.bfloat16),
        "gain_attn_out": jnp.clip(1.0 + 0.18 * jax.random.normal(splits[8], (D,), jnp.float32), 0.099609375, 1.8984375).astype(jnp.bfloat16),
        "gain_query": jnp.clip(1.0 + 0.18 * jax.random.normal(splits[9], (HD,), jnp.float32), 0.099609375, 1.8984375).astype(jnp.bfloat16),
        "gain_key": jnp.clip(1.0 + 0.18 * jax.random.normal(splits[10], (HD,), jnp.float32), 0.099609375, 1.8984375).astype(jnp.bfloat16),
        "gate_weight": bell_draw(splits[11], (D, FF), D ** -0.5, 0.1875, ((0, 16), (1, 2))),
        "up_weight": bell_draw(splits[12], (D, FF), D ** -0.5, 0.1875, ((0, 16), (1, 2))),
        "down_weight": bell_draw(splits[13], (D, FF), FF ** -0.5, 0.078125, ((0, 16), (1, 2))),
        "gain_ffn_in": jnp.clip(1.0 + 0.18 * jax.random.normal(splits[14], (D,), jnp.float32), 0.099609375, 1.8984375).astype(jnp.bfloat16),
        "gain_ffn_out": jnp.clip(1.0 + 0.18 * jax.random.normal(splits[15], (D,), jnp.float32), 0.099609375, 1.8984375).astype(jnp.bfloat16),
        "cotangent": bell_draw(splits[16], (TOKENS, D), 1.0, 6.0, ((0, 32),)),
    }


EPS = 1e-06
QUERY_SCALE = 0.0625
NEG_FILL = -1e+30
HIGH = lax.Precision.HIGHEST

@jax.custom_vjp
def low(v):
    return lax.optimization_barrier(v.astype(jnp.bfloat16)).astype(jnp.float32)

@jax.custom_vjp
def low_back(v):
    return v

def low_keep(v):
    return (low(v), None)

def low_pass(kept, grad):
    return (grad,)

def back_keep(v):
    return (v, None)

def back_low(kept, grad):
    return (low(grad),)
low.defvjp(low_keep, low_pass)
low_back.defvjp(back_keep, back_low)

def matmul_high(left, right):
    return jnp.dot(left, right, precision=HIGH, preferred_element_type=jnp.float32)

def rms_norm(values, norm_gain):
    return values * lax.rsqrt(lax.optimization_barrier(jnp.mean(values * values, axis=-1, keepdims=True)) + EPS) * norm_gain

def rotary_tables(positions, width):
    freq_steps = jnp.arange(width // 2, dtype=jnp.float32) * (2.0 / width)
    inverse = jnp.exp(freq_steps * -math.log(10000.0))
    phases = positions.astype(jnp.float32)[:, None] * inverse[None, :]
    return (jnp.cos(phases), jnp.sin(phases))

def rotate(values, cosine, sine):
    half_width = values.shape[-1] // 2
    first_half = values[..., :half_width]
    second = values[..., half_width:]
    return jnp.concatenate([first_half * cosine - second * sine, second * cosine + first_half * sine], axis=-1)

def reference(inputs, segments, positions, query_weight, key_weight, value_weight, output_weight, gain_attn_in, gain_attn_out, gain_query, gain_key, gate_weight, up_weight, down_weight, gain_ffn_in, gain_ffn_out, cotangent):
    cosine, sine = rotary_tables(positions.reshape(-1), HD)
    token_index = jnp.arange(SEQ)
    distance = token_index[:, None] - token_index[None, :]
    window_mask = (distance >= 0) & (distance < WINDOW)

    def attend(block):
        query_part, key_part, value_part, segment_row = block
        scores = low_back(jnp.einsum('thd,sd->hts', query_part, key_part, precision=HIGH))
        allowed = window_mask & (segment_row[:, None] == segment_row[None, :])
        scores = jnp.where(allowed[None], scores, NEG_FILL)
        probs = low(jax.nn.softmax(scores, axis=-1))
        return jnp.einsum('hts,sd->thd', probs, value_part, precision=HIGH)

    def forward(acts, w_query, w_key, w_value, w_output, g_attn_in, g_attn_out, g_query, g_key, w_gate, w_up, w_down, g_ffn_in, g_ffn_out):
        normed_attn = low(rms_norm(acts, g_attn_in))
        query_raw = low_back(matmul_high(normed_attn, w_query)).reshape(TOKENS, HEADS, HD)
        key_raw = low_back(matmul_high(normed_attn, w_key))
        value = low(low_back(matmul_high(normed_attn, w_value)))
        query = low(rotate(rms_norm(query_raw, g_query), cosine[:, None, :], sine[:, None, :]) * QUERY_SCALE)
        key = low(rotate(rms_norm(key_raw, g_key), cosine, sine))
        blocks = lax.map(jax.checkpoint(attend), (query.reshape(GROUPS, SEQ, HEADS, HD), key.reshape(GROUPS, SEQ, HD), value.reshape(GROUPS, SEQ, HD), segments))
        context = low(low_back(blocks.reshape(TOKENS, HEADS * HD)))
        branch_attn = low_back(jnp.einsum('tc,dc->td', context, w_output, precision=HIGH))
        hidden = acts + rms_norm(branch_attn, g_attn_out)
        normed_ffn = low(rms_norm(hidden, g_ffn_in))
        gate = low_back(matmul_high(normed_ffn, w_gate))
        upper = low_back(matmul_high(normed_ffn, w_up))
        activated = low(jax.nn.gelu(gate, approximate=True) * upper)
        branch_ffn = low_back(jnp.einsum('tf,df->td', activated, w_down, precision=HIGH))
        return hidden + rms_norm(branch_ffn, g_ffn_out)
    layer_out, pull = jax.vjp(forward, inputs.astype(jnp.float32), query_weight.astype(jnp.float32), key_weight.astype(jnp.float32), value_weight.astype(jnp.float32), output_weight.astype(jnp.float32), gain_attn_in.astype(jnp.float32), gain_attn_out.astype(jnp.float32), gain_query.astype(jnp.float32), gain_key.astype(jnp.float32), gate_weight.astype(jnp.float32), up_weight.astype(jnp.float32), down_weight.astype(jnp.float32), gain_ffn_in.astype(jnp.float32), gain_ffn_out.astype(jnp.float32))
    grads = pull(cotangent.astype(jnp.float32))
    return (layer_out.astype(jnp.bfloat16), grads[0], grads[1], grads[2], grads[3], grads[4], grads[5], grads[6], grads[7], grads[8], grads[9], grads[10], grads[11], grads[12], grads[13])
```

```python
import math

import jax
import jax.numpy as jnp
from jax import lax
from jax.sharding import PartitionSpec as P

WINDOW = 512


EPS = 1e-06
QUERY_SCALE = 0.0625
NEG_FILL = -1e30


def norm_rows(values, norm_gain):
    inv_rms = lax.rsqrt(jnp.mean(values * values, axis=-1, keepdims=True) + EPS)
    normed = values * inv_rms
    return (normed * norm_gain, normed, inv_rms)


def norm_back(gradient, normed, inv_rms, norm_gain):
    scaled_grad = gradient * norm_gain
    result = inv_rms * (
        scaled_grad - normed * jnp.mean(scaled_grad * normed, axis=-1, keepdims=True)
    )
    return (result, gradient * normed)


def rotary_tables(positions, width):
    freq_steps = jnp.arange(width // 2, dtype=jnp.float32) * (2.0 / width)
    inverse = jnp.exp(freq_steps * -math.log(10000.0))
    phases = positions.astype(jnp.float32)[:, None] * inverse[None, :]
    return (jnp.cos(phases), jnp.sin(phases))


def rotate(values, cosine, sine):
    half_width = values.shape[-1] // 2
    first_half = values[..., :half_width]
    second = values[..., half_width:]
    return jnp.concatenate(
        [first_half * cosine - second * sine, second * cosine + first_half * sine], axis=-1
    )


def gelu_product(gate_in, upper_in):
    return jax.nn.gelu(gate_in, approximate=True) * upper_in


def swap_pair(values):
    return lax.ppermute(values, "tensor", [(0, 1), (1, 0)])


def pair_rows(own):
    return jnp.concatenate([own, swap_pair(own)], axis=0)


def pair_sum(terms):
    half = terms.shape[0] // 2
    return terms[:half] + swap_pair(terms[half:].astype(jnp.bfloat16)).astype(jnp.float32)


def halving_sum(terms, order):
    count = lax.axis_size("dp")
    place = lax.axis_index("dp")
    bits = len(order)
    rows = terms.shape[0] // count
    total = terms.reshape((2,) * bits + (rows, terms.shape[1]))
    for bit in order:
        axis = bits - 1 - bit
        mine = (place >> bit) & 1
        kept = lax.dynamic_slice_in_dim(total, mine, 1, axis)
        sent = lax.dynamic_slice_in_dim(total, 1 - mine, 1, axis)
        got = lax.ppermute(sent, "dp", [(i, i ^ (1 << bit)) for i in range(count)])
        total = kept.astype(jnp.float32) + got.astype(jnp.float32)
        if bit != order[-1]:
            total = total.astype(jnp.bfloat16)
    return total.reshape(rows, terms.shape[1])


def column_plan(width):
    bits = lax.axis_size("dp").bit_length() - 1
    plain = tuple(range(bits))
    if bits < 3:
        return [(0, width, plain)]
    lanes = width // 128
    first = lanes * 2 // 5 * 128
    return [
        (0, first, plain),
        (first, 2 * first, (1, 0) + plain[2:]),
        (2 * first, width, plain[2:] + (0, 1)),
    ]


def row_scatter(terms):
    return jnp.concatenate(
        [halving_sum(terms[:, lo:hi], order) for lo, hi, order in column_plan(terms.shape[1])],
        axis=1,
    )


def grad_scatter(left, right):
    parts = []
    for lo, hi, order in column_plan(right.shape[1]):
        terms = jnp.einsum(
            "td,tf->df", left, right[:, lo:hi], preferred_element_type=jnp.float32
        ).astype(jnp.bfloat16)
        parts.append(halving_sum(terms, order))
    return jnp.concatenate(parts, axis=1)


def per_device(
    inputs,
    segments,
    positions,
    query_weight,
    key_weight,
    value_weight,
    output_weight,
    gain_attn_in,
    gain_attn_out,
    gain_query,
    gain_key,
    gate_weight,
    up_weight,
    down_weight,
    gain_ffn_in,
    gain_ffn_out,
    cotangent,
):
    half_rows = inputs.shape[0]
    side = lax.axis_index("tensor")
    count = lax.axis_size("dp")
    offset = side * half_rows
    head_dim = key_weight.shape[1]
    width = query_weight.shape[1]
    rows = query_weight.shape[0]
    head_rows = gain_query.shape[0]
    gain_columns = jnp.stack(
        [
            gain_attn_in,
            gain_attn_out,
            gain_ffn_in,
            gain_ffn_out,
            jnp.pad(gain_query, (0, rows - head_rows)),
            jnp.pad(gain_key, (0, rows - head_rows)),
        ],
        axis=1,
    )
    packed = jnp.concatenate(
        [
            query_weight,
            output_weight,
            key_weight,
            value_weight,
            jnp.pad(gain_columns, ((0, 0), (0, 122))),
        ],
        axis=1,
    )
    packed = lax.all_gather(packed, "dp", axis=0, tiled=True)
    query_weight = packed[:, :width]
    output_weight = packed[:, width : 2 * width]
    key_weight = packed[:, 2 * width : 2 * width + head_dim]
    value_weight = packed[:, 2 * width + head_dim : 2 * width + 2 * head_dim]
    gain_columns = packed[:, 2 * width + 2 * head_dim :]
    gain_attn_in, gain_attn_out, gain_ffn_in, gain_ffn_out = (
        gain_columns[:, i] for i in range(4)
    )
    gain_query, gain_key = (
        gain_columns[:, i].reshape(count, rows)[:, :head_rows].reshape(-1) for i in (4, 5)
    )
    gate_weight = lax.all_gather(gate_weight, "dp", axis=0, tiled=True)
    up_weight = lax.all_gather(up_weight, "dp", axis=0, tiled=True)
    down_weight = lax.all_gather(down_weight, "dp", axis=0, tiled=True)
    gain_attn_in = gain_attn_in.astype(jnp.float32)
    gain_attn_out = gain_attn_out.astype(jnp.float32)
    gain_query = gain_query.astype(jnp.float32)
    gain_key = gain_key.astype(jnp.float32)
    gain_ffn_in = gain_ffn_in.astype(jnp.float32)
    gain_ffn_out = gain_ffn_out.astype(jnp.float32)
    residual_in = inputs.astype(jnp.float32)
    attn_normed_in, attn_hat, attn_inv = norm_rows(residual_in, gain_attn_in)
    attn_local = attn_normed_in.astype(jnp.bfloat16)
    normed_rows = pair_rows(attn_local)
    seq_len = normed_rows.shape[0]

    def own_first(values):
        return jnp.concatenate(
            [
                lax.dynamic_slice_in_dim(values, offset, half_rows, 0),
                lax.dynamic_slice_in_dim(values, half_rows - offset, half_rows, 0),
            ]
        )

    token_index = own_first(jnp.arange(seq_len))
    documents = own_first(segments[0])
    cosine, sine = rotary_tables(own_first(positions[0]), head_dim)
    query_raw = jnp.dot(normed_rows, query_weight, preferred_element_type=jnp.float32)
    local_heads = query_raw.shape[1] // head_dim
    query_raw = query_raw.reshape(seq_len, local_heads, head_dim)
    key_raw = jnp.dot(normed_rows, key_weight, preferred_element_type=jnp.float32)
    value_low = jnp.dot(normed_rows, value_weight, preferred_element_type=jnp.float32).astype(
        jnp.bfloat16
    )
    query_normed, query_hat, query_inv = norm_rows(query_raw, gain_query)
    query_low = (rotate(query_normed, cosine[:, None, :], sine[:, None, :]) * QUERY_SCALE).astype(
        jnp.bfloat16
    )
    key_normed, key_hat, key_inv = norm_rows(key_raw, gain_key)
    key_low = rotate(key_normed, cosine, sine).astype(jnp.bfloat16)
    distance = token_index[:, None] - token_index[None, :]
    allowed = (documents[:, None] == documents[None, :]) & (distance >= 0) & (distance < WINDOW)
    scores = jnp.einsum("thd,sd->hts", query_low, key_low, preferred_element_type=jnp.float32)
    scores = jnp.where(allowed[None], scores, NEG_FILL)
    row_max = jnp.max(scores, axis=-1, keepdims=True)
    shifted = jnp.exp(scores - row_max)
    row_total = jnp.sum(shifted, axis=-1, keepdims=True)
    log_total = row_max + jnp.log(row_total)
    probs_low = (shifted / row_total).astype(jnp.bfloat16)
    context = jnp.einsum("hts,sd->thd", probs_low, value_low, preferred_element_type=jnp.float32)
    context = context.reshape(seq_len, local_heads * head_dim).astype(jnp.bfloat16)
    attn_terms = jnp.einsum("tc,dc->td", context, output_weight, preferred_element_type=jnp.float32)
    attn_branch = pair_sum(attn_terms)
    post_attn, post_attn_hat, post_attn_inv = norm_rows(attn_branch, gain_attn_out)
    hidden_in = residual_in + post_attn
    ffn_normed, ffn_hat, ffn_inv = norm_rows(hidden_in, gain_ffn_in)
    ffn_inputs = pair_rows(ffn_normed.astype(jnp.bfloat16))
    gate_pre = jnp.dot(ffn_inputs, gate_weight, preferred_element_type=jnp.float32)
    upper_pre = jnp.dot(ffn_inputs, up_weight, preferred_element_type=jnp.float32)
    activated, gelu_pull = jax.vjp(gelu_product, gate_pre, upper_pre)
    hidden_low = activated.astype(jnp.bfloat16)
    ffn_terms = jnp.einsum("tf,df->td", hidden_low, down_weight, preferred_element_type=jnp.float32)
    ffn_branch = pair_sum(ffn_terms)
    post_ffn, post_ffn_hat, post_ffn_inv = norm_rows(ffn_branch, gain_ffn_out)
    layer_out = (hidden_in + post_ffn).astype(jnp.bfloat16)
    out_grad = cotangent.astype(jnp.float32)
    ffn_branch_grad, gain_ffn_out_rows = norm_back(
        out_grad, post_ffn_hat, post_ffn_inv, gain_ffn_out
    )
    ffn_grad_all = pair_rows(ffn_branch_grad.astype(jnp.bfloat16))
    down_weight_grad = grad_scatter(ffn_grad_all, hidden_low)
    hidden_grad = jnp.dot(ffn_grad_all, down_weight, preferred_element_type=jnp.float32)
    gate_grad, upper_grad = gelu_pull(hidden_grad)
    gate_low = gate_grad.astype(jnp.bfloat16)
    upper_low = upper_grad.astype(jnp.bfloat16)
    gate_weight_grad = grad_scatter(ffn_inputs, gate_low)
    up_weight_grad = grad_scatter(ffn_inputs, upper_low)
    ffn_in_terms = jnp.einsum(
        "tf,df->td", gate_low, gate_weight, preferred_element_type=jnp.float32
    ) + jnp.einsum("tf,df->td", upper_low, up_weight, preferred_element_type=jnp.float32)
    ffn_in_grad = pair_sum(ffn_in_terms)
    ffn_norm_grad, gain_ffn_in_rows = norm_back(ffn_in_grad, ffn_hat, ffn_inv, gain_ffn_in)
    hidden_total = out_grad + ffn_norm_grad
    attn_branch_grad, gain_attn_out_rows = norm_back(
        hidden_total, post_attn_hat, post_attn_inv, gain_attn_out
    )
    branch_all = pair_rows(attn_branch_grad.astype(jnp.bfloat16))
    output_weight_grad = jnp.einsum(
        "td,tc->dc", branch_all, context, preferred_element_type=jnp.float32
    )
    context_grad = jnp.dot(branch_all, output_weight, preferred_element_type=jnp.float32)
    context_grad = context_grad.reshape(seq_len, local_heads, head_dim).astype(jnp.bfloat16)
    scores = jnp.einsum("thd,sd->hts", query_low, key_low, preferred_element_type=jnp.float32)
    scores = jnp.where(allowed[None], scores, NEG_FILL)
    probs = jnp.exp(scores - log_total)
    prob_grad = jnp.einsum(
        "thd,sd->hts", context_grad, value_low, preferred_element_type=jnp.float32
    )
    row_inner = jnp.sum(prob_grad * probs, axis=-1, keepdims=True)
    score_grad = (probs * (prob_grad - row_inner)).astype(jnp.bfloat16)
    value_grad = jnp.einsum(
        "hts,thd->sd", probs.astype(jnp.bfloat16), context_grad, preferred_element_type=jnp.float32
    )
    query_grad = (
        jnp.einsum("hts,sd->thd", score_grad, key_low, preferred_element_type=jnp.float32)
        * QUERY_SCALE
    )
    key_grad = jnp.einsum("hts,thd->sd", score_grad, query_low, preferred_element_type=jnp.float32)
    query_turned = rotate(query_grad, cosine[:, None, :], -sine[:, None, :])
    query_raw_grad, gain_query_parts = norm_back(query_turned, query_hat, query_inv, gain_query)
    gain_query_grad = jnp.sum(gain_query_parts, axis=(0, 1))
    query_raw_low = query_raw_grad.reshape(seq_len, local_heads * head_dim).astype(jnp.bfloat16)
    query_weight_grad = jnp.einsum(
        "td,tc->dc", normed_rows, query_raw_low, preferred_element_type=jnp.float32
    )
    input_terms = jnp.einsum(
        "tc,dc->td", query_raw_low, query_weight, preferred_element_type=jnp.float32
    )
    input_part = pair_sum(input_terms)
    key_part = pair_sum(key_grad)
    value_part = pair_sum(value_grad)
    local_cos, local_sin = cosine[:half_rows], sine[:half_rows]
    local_key_hat, local_key_inv = key_hat[:half_rows], key_inv[:half_rows]
    key_turned = rotate(key_part, local_cos, -local_sin)
    key_raw_grad, gain_key_rows = norm_back(key_turned, local_key_hat, local_key_inv, gain_key)
    key_raw_low = key_raw_grad.astype(jnp.bfloat16)
    value_raw_low = value_part.astype(jnp.bfloat16)
    key_weight_grad = jnp.einsum(
        "td,tc->dc", attn_local, key_raw_low, preferred_element_type=jnp.float32
    )
    value_weight_grad = jnp.einsum(
        "td,tc->dc", attn_local, value_raw_low, preferred_element_type=jnp.float32
    )
    normed_grad = (
        input_part
        + jnp.einsum("tc,dc->td", key_raw_low, key_weight, preferred_element_type=jnp.float32)
        + jnp.einsum("tc,dc->td", value_raw_low, value_weight, preferred_element_type=jnp.float32)
    )
    input_back, gain_attn_in_rows = norm_back(normed_grad, attn_hat, attn_inv, gain_attn_in)
    input_grad = hidden_total + input_back
    half_head_rows = head_rows // 2
    half_weight_rows = rows // 2

    def head_column(values):
        blocks = values.reshape(count, 2, half_head_rows)
        blocks = jnp.pad(blocks, ((0, 0), (0, 0), (0, half_weight_rows - half_head_rows)))
        return blocks.reshape(-1)

    gain_grads = jnp.stack(
        [
            jnp.sum(gain_attn_in_rows, axis=0),
            jnp.sum(gain_attn_out_rows, axis=0),
            jnp.sum(gain_ffn_in_rows, axis=0),
            jnp.sum(gain_ffn_out_rows, axis=0),
            head_column(gain_query_grad),
            head_column(jnp.sum(gain_key_rows, axis=0)),
        ],
        axis=1,
    )
    summed = row_scatter(
        jnp.concatenate(
            [
                query_weight_grad.astype(jnp.bfloat16),
                output_weight_grad.astype(jnp.bfloat16),
                key_weight_grad.astype(jnp.bfloat16),
                value_weight_grad.astype(jnp.bfloat16),
                jnp.pad(gain_grads, ((0, 0), (0, 122))).astype(jnp.bfloat16),
            ],
            axis=1,
        )
    )
    query_weight_grad = summed[:, :width]
    output_weight_grad = summed[:, width : 2 * width]
    shared = summed[:, 2 * width :]
    shared = lax.dynamic_slice_in_dim(
        shared, side * half_weight_rows, half_weight_rows, 0
    ) + swap_pair(
        lax.dynamic_slice_in_dim(shared, (1 - side) * half_weight_rows, half_weight_rows, 0)
    )
    key_weight_grad = shared[:, :head_dim]
    value_weight_grad = shared[:, head_dim : 2 * head_dim]
    gain_grads = shared[:, 2 * head_dim :]
    gain_attn_in_grad, gain_attn_out_grad, gain_ffn_in_grad, gain_ffn_out_grad = (
        gain_grads[:, i] for i in range(4)
    )
    gain_query_grad, gain_key_grad = (gain_grads[:half_head_rows, i] for i in (4, 5))
    return (
        layer_out,
        input_grad,
        query_weight_grad,
        key_weight_grad,
        value_weight_grad,
        output_weight_grad,
        gain_attn_in_grad,
        gain_attn_out_grad,
        gain_query_grad,
        gain_key_grad,
        gate_weight_grad,
        up_weight_grad,
        down_weight_grad,
        gain_ffn_in_grad,
        gain_ffn_out_grad,
    )


def solution(mesh):
    in_specs = (
        P(("dp", "tensor"), None),
        P("dp", None),
        P("dp", None),
        P("dp", "tensor"),
        P("dp", None),
        P("dp", None),
        P("dp", "tensor"),
        P("dp"),
        P("dp"),
        P("dp"),
        P("dp"),
        P("dp", "tensor"),
        P("dp", "tensor"),
        P("dp", "tensor"),
        P("dp"),
        P("dp"),
        P(("dp", "tensor"), None),
    )
    out_specs = (
        P(("dp", "tensor"), None),
        P(("dp", "tensor"), None),
        P("dp", "tensor"),
        P(("dp", "tensor"), None),
        P(("dp", "tensor"), None),
        P("dp", "tensor"),
        P(("dp", "tensor")),
        P(("dp", "tensor")),
        P(("dp", "tensor")),
        P(("dp", "tensor")),
        P("dp", "tensor"),
        P("dp", "tensor"),
        P("dp", "tensor"),
        P(("dp", "tensor")),
        P(("dp", "tensor")),
    )
    return jax.shard_map(
        per_device, mesh=mesh, in_specs=in_specs, out_specs=out_specs, check_vma=False
    )
```

```python
import math

import jax
import jax.numpy as jnp
from jax import lax
from jax.sharding import PartitionSpec as P

WINDOW = 512


EPS = 1e-06
QUERY_SCALE = 0.0625
NEG_FILL = -1e30


def norm_rows(values, norm_gain):
    inv_rms = lax.rsqrt(jnp.mean(values * values, axis=-1, keepdims=True) + EPS)
    normed = values * inv_rms
    return (normed * norm_gain, normed, inv_rms)


def norm_back(gradient, normed, inv_rms, norm_gain):
    scaled_grad = gradient * norm_gain
    result = inv_rms * (
        scaled_grad - normed * jnp.mean(scaled_grad * normed, axis=-1, keepdims=True)
    )
    return (result, gradient * normed)


def rotary_tables(positions, width):
    freq_steps = jnp.arange(width // 2, dtype=jnp.float32) * (2.0 / width)
    inverse = jnp.exp(freq_steps * -math.log(10000.0))
    phases = positions.astype(jnp.float32)[:, None] * inverse[None, :]
    return (jnp.cos(phases), jnp.sin(phases))


def rotate(values, cosine, sine):
    half_width = values.shape[-1] // 2
    first_half = values[..., :half_width]
    second = values[..., half_width:]
    return jnp.concatenate(
        [first_half * cosine - second * sine, second * cosine + first_half * sine], axis=-1
    )


def gelu_product(gate_in, upper_in):
    return jax.nn.gelu(gate_in, approximate=True) * upper_in


def swap_pair(values):
    return lax.ppermute(values, "tensor", [(0, 1), (1, 0)])


def pair_rows(own):
    return jnp.concatenate([own, swap_pair(own)], axis=0)


def pair_sum(terms):
    half = terms.shape[0] // 2
    return terms[:half] + swap_pair(terms[half:].astype(jnp.bfloat16)).astype(jnp.float32)


def halving_sum(terms, order, after=None):
    count = lax.axis_size("dp")
    place = lax.axis_index("dp")
    bits = len(order)
    rows = terms.shape[0] // count
    total = terms.reshape((2,) * bits + (rows, terms.shape[1]))
    for bit in order:
        axis = bits - 1 - bit
        mine = (place >> bit) & 1
        kept = lax.dynamic_slice_in_dim(total, mine, 1, axis)
        sent = lax.dynamic_slice_in_dim(total, 1 - mine, 1, axis)
        got = lax.ppermute(sent, "dp", [(i, i ^ (1 << bit)) for i in range(count)])
        total = kept.astype(jnp.float32) + got.astype(jnp.float32)
        if after is not None and bit == order[0]:
            total = total + after
        if bit != order[-1]:
            total = total.astype(jnp.bfloat16)
    return total.reshape(rows, terms.shape[1])


def column_plan(width):
    bits = lax.axis_size("dp").bit_length() - 1
    plain = tuple(range(bits))
    if bits < 3:
        return [(0, width, plain)]
    lanes = width // 128
    first = lanes * 2 // 5 * 128
    return [
        (0, first, plain),
        (first, 2 * first, (1, 0) + plain[2:]),
        (2 * first, width, plain[2:] + (0, 1)),
    ]


def row_scatter(terms):
    return jnp.concatenate(
        [halving_sum(terms[:, lo:hi], order) for lo, hi, order in column_plan(terms.shape[1])],
        axis=1,
    )


def grad_scatter(left, right, after=None):
    parts = []
    for lo, hi, order in column_plan(right.shape[1]):
        terms = jnp.einsum(
            "td,tf->df", left, right[:, lo:hi], preferred_element_type=jnp.float32
        ).astype(jnp.bfloat16)
        parts.append(halving_sum(terms, order, after))
    return jnp.concatenate(parts, axis=1)


def per_device(
    inputs,
    segments,
    positions,
    query_weight,
    key_weight,
    value_weight,
    output_weight,
    gain_attn_in,
    gain_attn_out,
    gain_query,
    gain_key,
    gate_weight,
    up_weight,
    down_weight,
    gain_ffn_in,
    gain_ffn_out,
    cotangent,
):
    half_rows = inputs.shape[0]
    side = lax.axis_index("tensor")
    count = lax.axis_size("dp")
    offset = side * half_rows
    head_dim = key_weight.shape[1]
    width = query_weight.shape[1]
    rows = query_weight.shape[0]
    head_rows = gain_query.shape[0]
    gain_columns = jnp.stack(
        [
            gain_attn_in,
            gain_attn_out,
            gain_ffn_in,
            gain_ffn_out,
            jnp.pad(gain_query, (0, rows - head_rows)),
            jnp.pad(gain_key, (0, rows - head_rows)),
        ],
        axis=1,
    )
    packed = jnp.concatenate(
        [
            query_weight,
            output_weight,
            key_weight,
            value_weight,
            jnp.pad(gain_columns, ((0, 0), (0, 122))),
        ],
        axis=1,
    )
    packed = lax.all_gather(packed, "dp", axis=0, tiled=True)
    query_weight = packed[:, :width]
    output_weight = packed[:, width : 2 * width]
    key_weight = packed[:, 2 * width : 2 * width + head_dim]
    value_weight = packed[:, 2 * width + head_dim : 2 * width + 2 * head_dim]
    gain_columns = packed[:, 2 * width + 2 * head_dim :]
    gain_attn_in, gain_attn_out, gain_ffn_in, gain_ffn_out = (
        gain_columns[:, i] for i in range(4)
    )
    gain_query, gain_key = (
        gain_columns[:, i].reshape(count, rows)[:, :head_rows].reshape(-1) for i in (4, 5)
    )
    units = gate_weight.shape[1]
    gate_up = lax.all_gather(
        jnp.concatenate([gate_weight, up_weight], axis=1), "dp", axis=0, tiled=True
    )
    gate_weight, up_weight = gate_up[:, :units], gate_up[:, units:]
    down_weight = lax.all_gather(down_weight, "dp", axis=0, tiled=True)
    gain_attn_in = gain_attn_in.astype(jnp.float32)
    gain_attn_out = gain_attn_out.astype(jnp.float32)
    gain_query = gain_query.astype(jnp.float32)
    gain_key = gain_key.astype(jnp.float32)
    gain_ffn_in = gain_ffn_in.astype(jnp.float32)
    gain_ffn_out = gain_ffn_out.astype(jnp.float32)
    residual_in = inputs.astype(jnp.float32)
    attn_normed_in, attn_hat, attn_inv = norm_rows(residual_in, gain_attn_in)
    attn_local = attn_normed_in.astype(jnp.bfloat16)
    normed_rows = pair_rows(attn_local)
    seq_len = normed_rows.shape[0]

    def own_first(values):
        return jnp.concatenate(
            [
                lax.dynamic_slice_in_dim(values, offset, half_rows, 0),
                lax.dynamic_slice_in_dim(values, half_rows - offset, half_rows, 0),
            ]
        )

    token_index = own_first(jnp.arange(seq_len))
    documents = own_first(segments[0])
    cosine, sine = rotary_tables(own_first(positions[0]), head_dim)
    query_raw = jnp.dot(normed_rows, query_weight, preferred_element_type=jnp.float32)
    local_heads = query_raw.shape[1] // head_dim
    query_raw = query_raw.reshape(seq_len, local_heads, head_dim)
    key_raw = jnp.dot(normed_rows, key_weight, preferred_element_type=jnp.float32)
    value_low = jnp.dot(normed_rows, value_weight, preferred_element_type=jnp.float32).astype(
        jnp.bfloat16
    )
    query_normed, query_hat, query_inv = norm_rows(query_raw, gain_query)
    query_low = (rotate(query_normed, cosine[:, None, :], sine[:, None, :]) * QUERY_SCALE).astype(
        jnp.bfloat16
    )
    key_normed, key_hat, key_inv = norm_rows(key_raw, gain_key)
    key_low = rotate(key_normed, cosine, sine).astype(jnp.bfloat16)
    distance = token_index[:, None] - token_index[None, :]
    allowed = (documents[:, None] == documents[None, :]) & (distance >= 0) & (distance < WINDOW)
    scores = jnp.einsum("thd,sd->hts", query_low, key_low, preferred_element_type=jnp.float32)
    scores = jnp.where(allowed[None], scores, NEG_FILL)
    row_max = jnp.max(scores, axis=-1, keepdims=True)
    shifted = jnp.exp(scores - row_max)
    row_total = jnp.sum(shifted, axis=-1, keepdims=True)
    log_total = row_max + jnp.log(row_total)
    probs_low = (shifted / row_total).astype(jnp.bfloat16)
    context = jnp.einsum("hts,sd->thd", probs_low, value_low, preferred_element_type=jnp.float32)
    context = context.reshape(seq_len, local_heads * head_dim).astype(jnp.bfloat16)
    attn_terms = jnp.einsum("tc,dc->td", context, output_weight, preferred_element_type=jnp.float32)
    attn_branch = pair_sum(attn_terms)
    post_attn, post_attn_hat, post_attn_inv = norm_rows(attn_branch, gain_attn_out)
    hidden_in = residual_in + post_attn
    ffn_normed, ffn_hat, ffn_inv = norm_rows(hidden_in, gain_ffn_in)
    ffn_inputs = pair_rows(ffn_normed.astype(jnp.bfloat16))
    gate_pre = jnp.dot(ffn_inputs, gate_weight, preferred_element_type=jnp.float32)
    upper_pre = jnp.dot(ffn_inputs, up_weight, preferred_element_type=jnp.float32)
    activated, gelu_pull = jax.vjp(gelu_product, gate_pre, upper_pre)
    hidden_low = activated.astype(jnp.bfloat16)
    ffn_terms = jnp.einsum("tf,df->td", hidden_low, down_weight, preferred_element_type=jnp.float32)
    ffn_branch = pair_sum(ffn_terms)
    post_ffn, post_ffn_hat, post_ffn_inv = norm_rows(ffn_branch, gain_ffn_out)
    layer_out = (hidden_in + post_ffn).astype(jnp.bfloat16)
    out_grad = cotangent.astype(jnp.float32)
    ffn_branch_grad, gain_ffn_out_rows = norm_back(
        out_grad, post_ffn_hat, post_ffn_inv, gain_ffn_out
    )
    ffn_grad_all = pair_rows(ffn_branch_grad.astype(jnp.bfloat16))
    down_weight_grad = grad_scatter(ffn_grad_all, hidden_low)
    hidden_grad = jnp.dot(ffn_grad_all, down_weight, preferred_element_type=jnp.float32)
    gate_grad, upper_grad = gelu_pull(hidden_grad)
    gate_low = gate_grad.astype(jnp.bfloat16)
    upper_low = upper_grad.astype(jnp.bfloat16)
    ffn_in_terms = jnp.einsum(
        "tf,df->td", gate_low, gate_weight, preferred_element_type=jnp.float32
    ) + jnp.einsum("tf,df->td", upper_low, up_weight, preferred_element_type=jnp.float32)
    ffn_in_grad = pair_sum(ffn_in_terms)
    ffn_norm_grad, gain_ffn_in_rows = norm_back(ffn_in_grad, ffn_hat, ffn_inv, gain_ffn_in)
    hidden_total = out_grad + ffn_norm_grad
    attn_branch_grad, gain_attn_out_rows = norm_back(
        hidden_total, post_attn_hat, post_attn_inv, gain_attn_out
    )
    branch_all = pair_rows(attn_branch_grad.astype(jnp.bfloat16))
    output_weight_grad = jnp.einsum(
        "td,tc->dc", branch_all, context, preferred_element_type=jnp.float32
    )
    context_grad = jnp.dot(branch_all, output_weight, preferred_element_type=jnp.float32)
    context_grad = context_grad.reshape(seq_len, local_heads, head_dim).astype(jnp.bfloat16)
    scores = jnp.einsum("thd,sd->hts", query_low, key_low, preferred_element_type=jnp.float32)
    scores = jnp.where(allowed[None], scores, NEG_FILL)
    probs = jnp.exp(scores - log_total)
    prob_grad = jnp.einsum(
        "thd,sd->hts", context_grad, value_low, preferred_element_type=jnp.float32
    )
    row_inner = jnp.sum(prob_grad * probs, axis=-1, keepdims=True)
    score_grad = (probs * (prob_grad - row_inner)).astype(jnp.bfloat16)
    value_grad = jnp.einsum(
        "hts,thd->sd", probs.astype(jnp.bfloat16), context_grad, preferred_element_type=jnp.float32
    )
    query_grad = (
        jnp.einsum("hts,sd->thd", score_grad, key_low, preferred_element_type=jnp.float32)
        * QUERY_SCALE
    )
    key_grad = jnp.einsum("hts,thd->sd", score_grad, query_low, preferred_element_type=jnp.float32)
    query_turned = rotate(query_grad, cosine[:, None, :], -sine[:, None, :])
    query_raw_grad, gain_query_parts = norm_back(query_turned, query_hat, query_inv, gain_query)
    gain_query_grad = jnp.sum(gain_query_parts, axis=(0, 1))
    query_raw_low = query_raw_grad.reshape(seq_len, local_heads * head_dim).astype(jnp.bfloat16)
    gate_weight_grad = grad_scatter(
        ffn_inputs, gate_low, score_grad[0, 0, 0].astype(jnp.float32) * 0.0
    )
    up_weight_grad = grad_scatter(
        ffn_inputs, upper_low, query_raw_low[0, 0].astype(jnp.float32) * 0.0
    )
    query_weight_grad = jnp.einsum(
        "td,tc->dc", normed_rows, query_raw_low, preferred_element_type=jnp.float32
    )
    input_terms = jnp.einsum(
        "tc,dc->td", query_raw_low, query_weight, preferred_element_type=jnp.float32
    )
    input_part = pair_sum(input_terms)
    key_part = pair_sum(key_grad)
    value_part = pair_sum(value_grad)
    local_cos, local_sin = cosine[:half_rows], sine[:half_rows]
    local_key_hat, local_key_inv = key_hat[:half_rows], key_inv[:half_rows]
    key_turned = rotate(key_part, local_cos, -local_sin)
    key_raw_grad, gain_key_rows = norm_back(key_turned, local_key_hat, local_key_inv, gain_key)
    key_raw_low = key_raw_grad.astype(jnp.bfloat16)
    value_raw_low = value_part.astype(jnp.bfloat16)
    key_weight_grad = jnp.einsum(
        "td,tc->dc", attn_local, key_raw_low, preferred_element_type=jnp.float32
    )
    value_weight_grad = jnp.einsum(
        "td,tc->dc", attn_local, value_raw_low, preferred_element_type=jnp.float32
    )
    normed_grad = (
        input_part
        + jnp.einsum("tc,dc->td", key_raw_low, key_weight, preferred_element_type=jnp.float32)
        + jnp.einsum("tc,dc->td", value_raw_low, value_weight, preferred_element_type=jnp.float32)
    )
    input_back, gain_attn_in_rows = norm_back(normed_grad, attn_hat, attn_inv, gain_attn_in)
    input_grad = hidden_total + input_back
    half_head_rows = head_rows // 2
    half_weight_rows = rows // 2

    def head_column(values):
        blocks = values.reshape(count, 2, half_head_rows)
        blocks = jnp.pad(blocks, ((0, 0), (0, 0), (0, half_weight_rows - half_head_rows)))
        return blocks.reshape(-1)

    gain_grads = jnp.stack(
        [
            jnp.sum(gain_attn_in_rows, axis=0),
            jnp.sum(gain_attn_out_rows, axis=0),
            jnp.sum(gain_ffn_in_rows, axis=0),
            jnp.sum(gain_ffn_out_rows, axis=0),
            head_column(gain_query_grad),
            head_column(jnp.sum(gain_key_rows, axis=0)),
        ],
        axis=1,
    )
    summed = row_scatter(
        jnp.concatenate(
            [
                query_weight_grad.astype(jnp.bfloat16),
                output_weight_grad.astype(jnp.bfloat16),
                key_weight_grad.astype(jnp.bfloat16),
                value_weight_grad.astype(jnp.bfloat16),
                jnp.pad(gain_grads, ((0, 0), (0, 122))).astype(jnp.bfloat16),
            ],
            axis=1,
        )
    )
    query_weight_grad = summed[:, :width]
    output_weight_grad = summed[:, width : 2 * width]
    shared = summed[:, 2 * width :]
    shared = lax.dynamic_slice_in_dim(
        shared, side * half_weight_rows, half_weight_rows, 0
    ) + swap_pair(
        lax.dynamic_slice_in_dim(shared, (1 - side) * half_weight_rows, half_weight_rows, 0)
    )
    key_weight_grad = shared[:, :head_dim]
    value_weight_grad = shared[:, head_dim : 2 * head_dim]
    gain_grads = shared[:, 2 * head_dim :]
    gain_attn_in_grad, gain_attn_out_grad, gain_ffn_in_grad, gain_ffn_out_grad = (
        gain_grads[:, i] for i in range(4)
    )
    gain_query_grad, gain_key_grad = (gain_grads[:half_head_rows, i] for i in (4, 5))
    return (
        layer_out,
        input_grad,
        query_weight_grad,
        key_weight_grad,
        value_weight_grad,
        output_weight_grad,
        gain_attn_in_grad,
        gain_attn_out_grad,
        gain_query_grad,
        gain_key_grad,
        gate_weight_grad,
        up_weight_grad,
        down_weight_grad,
        gain_ffn_in_grad,
        gain_ffn_out_grad,
    )


def solution(mesh):
    in_specs = (
        P(("dp", "tensor"), None),
        P("dp", None),
        P("dp", None),
        P("dp", "tensor"),
        P("dp", None),
        P("dp", None),
        P("dp", "tensor"),
        P("dp"),
        P("dp"),
        P("dp"),
        P("dp"),
        P("dp", "tensor"),
        P("dp", "tensor"),
        P("dp", "tensor"),
        P("dp"),
        P("dp"),
        P(("dp", "tensor"), None),
    )
    out_specs = (
        P(("dp", "tensor"), None),
        P(("dp", "tensor"), None),
        P("dp", "tensor"),
        P(("dp", "tensor"), None),
        P(("dp", "tensor"), None),
        P("dp", "tensor"),
        P(("dp", "tensor")),
        P(("dp", "tensor")),
        P(("dp", "tensor")),
        P(("dp", "tensor")),
        P("dp", "tensor"),
        P("dp", "tensor"),
        P("dp", "tensor"),
        P(("dp", "tensor")),
        P(("dp", "tensor")),
    )
    return jax.shard_map(
        per_device, mesh=mesh, in_specs=in_specs, out_specs=out_specs, check_vma=False
    )
```
